32 devices in a mesh: zonal: 4 (over y, x), deg: 8 (over z, core).
Axes of the slice: x: 2, y: 2, z: 4, core: 2. Of those that a mesh axis runs over, the one named last changes fastest.
Arguments:
- spectral: bfloat16 [128, 2560, 128], P('zonal', 'deg'), may hold values from -6 to 6
- wavenumbers: int32 [128], P('zonal'), may hold values from 0 to 2559, as said below
- compress: bfloat16 [128, 2560, 128], P('zonal', 'deg'), may hold values from -0.3125 to 0.3125
- section_own: bfloat16 [2, 128, 8, 128, 128], P(None, 'zonal', 'deg'), may hold values from -0.375 to 0.375
- section_peer: bfloat16 [2, 128, 8, 128, 128], P(None, 'zonal', 'deg'), may hold values from -0.375 to 0.375
- expand: bfloat16 [128, 8, 640, 128], P('zonal', 'deg'), may hold values from -0.5 to 0.5
- block_ranks: int32 [3, 8], replicated, may hold values from 64 to 128, as said below
Outputs:
- fourier_rows: bfloat16 [128, 8, 4, 80, 128], P(None, 'deg', 'zonal')
The draws below stay inside these ranges and needn't reach their ends.
Inputs may be any that keep to these rules, and one draw needn't show every extreme that they name: Distinct wavenumbers, sorted and dealt to the 4 groups of 32 slots in rounds of 8: one slot to each group going forward through the groups, then one to each going backward; 0 and 2559 always appear. block_ranks[s, g] is the live rank of block g after section s; in each section some block has rank 128.
All inputs are finite; a program needn't handle non-finite values.
Results may differ from the reference program's by a relative error of at most 0.008.
Values may be sent and summed in bfloat16 or wider, within the bound.
No kernel may reach another device: no remote copies, remote signals or barrier semaphores. Data moves between devices by JAX's collectives and lax.ppermute only.
A program may use at most 128 MiB of HBM per device.

```python
import jax
import jax.numpy as jnp
from jax import lax

NDEG = 2560
K = 128
SECTIONS = 2
M_DEV = 32
BLOCKS = 8
ZONES = 4
NB = 320
QUART = 640
GLOW = 2
PIECE = 80
M_ALL = 128
COLS = 128


def draw_wavenumbers(key, part):
    key = jax.random.fold_in(key, 5)
    inner_values = jax.random.permutation(key, NDEG - 2)[:M_ALL - 2].astype(jnp.int32) + 1
    chosen = jnp.sort(jnp.concatenate([jnp.array([0, NDEG - 1], dtype=jnp.int32), inner_values]))
    sorted_rank = jnp.arange(M_ALL, dtype=jnp.int32)
    round_length = 2 * ZONES
    round_phase = sorted_rank % round_length
    group_index = jnp.where(round_phase < ZONES, round_phase, round_length - 1 - round_phase)
    slot_index = sorted_rank // round_length * 2 + (round_phase >= ZONES).astype(jnp.int32)
    placement = group_index * M_DEV + slot_index
    return jnp.zeros((M_ALL,), jnp.int32).at[placement].set(chosen)


def draw_block_ranks(key, part):
    key = jax.random.fold_in(key, 11)
    first_key, second_key = jax.random.split(key)
    values = jax.random.randint(first_key, (SECTIONS + 1, BLOCKS), K // 2, K + 1)
    full_at = jax.random.randint(second_key, (SECTIONS + 1, 1), 0, BLOCKS)
    chosen = jnp.arange(BLOCKS)[None, :] == full_at
    return jnp.where(chosen, K, values).astype(jnp.int32)


def block_levels(stream_key, extent, cuts, smallest, top_value):
    loudness = 1.0
    for position, shards_of in cuts:
        steps = jax.random.uniform(jax.random.fold_in(jax.random.fold_in(stream_key, 6), position), (shards_of,), jnp.float32, smallest / len(cuts), top_value / len(cuts))
        loudness = loudness * jnp.repeat(jnp.exp(steps), extent[position] // shards_of).reshape((-1,) + (1,) * (len(extent) - 1 - position))
    return loudness


def noise(own_key, shape, spread, reach, shards=(), held_as=jnp.bfloat16):
    entries = spread * jax.random.normal(own_key, shape, jnp.float32)
    if shards:
        entries = entries * block_levels(own_key, shape, shards, -0.22, 0.18)
    return jnp.clip(entries, -reach, reach).astype(held_as)


def setup_inputs(seed: int = 0) -> dict:
    key_list = jax.random.split(jax.random.key(seed), 8)
    return {
        "spectral": noise(key_list[0], (M_ALL, NDEG, COLS), 1.0, 6.0, ((0, 4), (1, 8))),
        "wavenumbers": draw_wavenumbers(jax.random.fold_in(key_list[7], 71), 0),
        "compress": noise(key_list[2], (M_ALL, NDEG, K), NB ** -0.5, 0.3125, ((0, 4), (1, 8))),
        "section_own": noise(key_list[3], (SECTIONS, M_ALL, BLOCKS, K, K), (2 * K) ** -0.5, 0.375, ((1, 4), (2, 8))),
        "section_peer": noise(key_list[4], (SECTIONS, M_ALL, BLOCKS, K, K), (2 * K) ** -0.5, 0.375, ((1, 4), (2, 8))),
        "expand": noise(key_list[5], (M_ALL, BLOCKS, QUART, K), K ** -0.5, 0.5, ((0, 4), (1, 8))),
        "block_ranks": draw_block_ranks(jax.random.fold_in(key_list[7], 71), 0),
    }


def reference(spectral, wavenumbers, compress, section_own, section_peer, expand, block_ranks):
    block_size = NDEG // BLOCKS
    positions = jnp.arange(BLOCKS, dtype=jnp.int32)
    keep_masks = (jnp.arange(K, dtype=jnp.int32)[None, None, :] < block_ranks[:, :, None]).astype(jnp.float32)
    degrees = jnp.arange(NDEG, dtype=jnp.int32)
    slot_ids = jnp.arange(M_ALL, dtype=jnp.int32)

    def one_slot(operand_pair):
        coeff_rows, wavenumber, squeeze_w, expand_w, slot_id = operand_pair
        local_weight = lax.dynamic_index_in_dim(section_own, slot_id, 1, keepdims=False)
        counterpart_weight = lax.dynamic_index_in_dim(section_peer, slot_id, 1, keepdims=False)
        live_rows = jnp.where((degrees >= wavenumber)[:, None], coeff_rows, jnp.zeros_like(coeff_rows))
        merged_result = jnp.einsum("gnk,gnc->gkc", squeeze_w.reshape(BLOCKS, block_size, K).astype(jnp.float32), live_rows.reshape(BLOCKS, block_size, COLS).astype(jnp.float32))
        vectors = (merged_result * keep_masks[0][:, :, None]).astype(jnp.bfloat16)
        for section_ordinal in range(1, SECTIONS + 1):
            counterpart = jnp.bitwise_xor(positions, BLOCKS >> section_ordinal)
            present_values = vectors.astype(jnp.float32)
            merged_result = jnp.einsum("xbz,xzi->xbi", local_weight[section_ordinal - 1].astype(jnp.float32), present_values)
            merged_result = merged_result + jnp.einsum("xbz,xzi->xbi", counterpart_weight[section_ordinal - 1].astype(jnp.float32), present_values[counterpart])
            vectors = (merged_result * keep_masks[section_ordinal][:, :, None]).astype(jnp.bfloat16)
        partial_rows = jnp.einsum("grk,gkc->grc", expand_w.astype(jnp.float32), vectors.astype(jnp.float32))
        summed = partial_rows.reshape(2 ** SECTIONS, GLOW, QUART, COLS).sum(axis=1)
        return summed.reshape(BLOCKS, ZONES, PIECE, COLS).astype(jnp.bfloat16)

    return lax.map(one_slot, (spectral, wavenumbers, compress, expand, slot_ids))
```

```python
import functools

import jax
import jax.numpy as jnp
from jax import lax
from jax.experimental import pallas as pl
from jax.experimental.pallas import tpu as pltpu
from jax.sharding import PartitionSpec as P

SECTIONS = 2
CHUNKS = (8, 8, 8, 4, 4)
VMEM_LIMIT = 32 * 2**20


def from_partner(array, axis, offset):
    pairs = [(i, i ^ offset) for i in range(lax.axis_size(axis))]
    return lax.ppermute(array, axis, pairs)


def dot(a, b, contract_a=1):
    return lax.dot_general(
        a, b, (((contract_a,), (0,)), ((), ())), preferred_element_type=jnp.float32
    )


def call(kernel, name, scalars, operands, in_specs, out_specs, out_shape, steps, flops):
    outs = out_shape if isinstance(out_shape, (list, tuple)) else [out_shape]
    moved = sum(o.size * o.dtype.itemsize for o in outs) + flops // 128
    return pl.pallas_call(
        kernel,
        out_shape=out_shape,
        grid_spec=pltpu.PrefetchScalarGridSpec(
            num_scalar_prefetch=len(scalars),
            grid=(steps,),
            in_specs=in_specs,
            out_specs=out_specs,
        ),
        compiler_params=pltpu.CompilerParams(vmem_limit_bytes=VMEM_LIMIT),
        cost_estimate=pl.CostEstimate(flops=flops, bytes_accessed=moved, transcendentals=0),
        name=name,
    )(*scalars, *operands)


def group(count):
    return max(b for b in (4, 2, 1) if count % b == 0)


def compress_kernel(first, b, waves, ranks, x_ref, a_ref, o_ref):
    block = lax.axis_index("deg")
    step = pl.program_id(0)
    nb, cols = x_ref.shape[1:]
    width = a_ref.shape[2]
    degree = lax.broadcasted_iota(jnp.int32, (nb, cols), 0) + block * nb
    keep = lax.broadcasted_iota(jnp.int32, (width, cols), 0) < ranks[0, block]
    for j in range(b):
        live = jnp.where(degree >= waves[first + step * b + j], x_ref[j], 0).astype(x_ref.dtype)
        total = dot(a_ref[j], live, 0)
        o_ref[j] = jnp.where(keep, total, 0.0).astype(o_ref.dtype)


def compress_slots(first, count, waves, ranks, spectral, compress):
    b = group(count)
    nb, cols = spectral.shape[1:]
    width = compress.shape[2]
    start = first // b
    return call(
        functools.partial(compress_kernel, first, b),
        "compress_slots",
        (waves, ranks),
        (spectral, compress),
        [
            pl.BlockSpec((b, nb, cols), lambda i, *_: (start + i, 0, 0)),
            pl.BlockSpec((b, nb, width), lambda i, *_: (start + i, 0, 0)),
        ],
        pl.BlockSpec((b, width, cols), lambda i, *_: (i, 0, 0)),
        jax.ShapeDtypeStruct((count, width, cols), jnp.bfloat16),
        count // b,
        2 * count * nb * width * cols,
    )


def section_kernel(section, b, ranks, own_ref, peer_ref, v_ref, u_ref, o_ref):
    block = lax.axis_index("deg")
    width, cols = v_ref.shape[1:]
    keep = lax.broadcasted_iota(jnp.int32, (width, cols), 0) < ranks[section, block]
    for j in range(b):
        total = dot(own_ref[j], v_ref[j]) + dot(peer_ref[j], u_ref[j])
        o_ref[j] = jnp.where(keep, total, 0.0).astype(o_ref.dtype)


def section_slots(section, first, ranks, own, peer, vector, partner):
    count, width, cols = vector.shape
    b = group(count)
    start = first // b
    weight = pl.BlockSpec(
        (None, b, None, width, width), lambda i, *_: (section - 1, start + i, 0, 0, 0)
    )
    part = pl.BlockSpec((b, width, cols), lambda i, *_: (i, 0, 0))
    return call(
        functools.partial(section_kernel, section, b),
        f"section_{section}_slots",
        (ranks,),
        (own, peer, vector, partner),
        [weight, weight, part, part],
        part,
        jax.ShapeDtypeStruct(vector.shape, jnp.bfloat16),
        count // b,
        4 * count * width * width * cols,
    )


def expand_kernel(b, pieces, place, kept_ref, got_ref, v_ref, u_ref, *refs):
    outs, rows_ref = refs[:-1], refs[-1]
    piece = outs[0].shape[1]
    zone = lax.axis_index("zonal")
    for j in range(b):
        total = dot(kept_ref[j], v_ref[j]) + dot(got_ref[j], u_ref[j])
        rows_ref[...] = total
        for offset in range(pieces):
            at = pl.multiple_of((zone ^ offset) * piece, piece)
            outs[offset][j] = rows_ref[pl.ds(at, piece), :].astype(outs[offset].dtype)


def expand_pieces(first, place, expand, got, vector, partner, pieces):
    count, width, cols = vector.shape
    rows = got.shape[1]
    piece = rows // pieces
    b = group(count)
    start = first // b
    part = pl.BlockSpec((b, width, cols), lambda i, *_: (i, 0, 0))
    moved = pl.BlockSpec((b, piece, cols), lambda i, *_: (i, 0, 0))
    flops = 4 * count * rows * width * cols
    return pl.pallas_call(
        functools.partial(expand_kernel, b, pieces),
        out_shape=[jax.ShapeDtypeStruct((count, piece, cols), jnp.bfloat16)] * pieces,
        grid_spec=pltpu.PrefetchScalarGridSpec(
            num_scalar_prefetch=1,
            grid=(count // b,),
            in_specs=[
                pl.BlockSpec((b, None, rows, width), lambda i, p: (start + i, 0, p[0], 0)),
                pl.BlockSpec((b, rows, width), lambda i, p: (start + i, 0, 0)),
                part,
                part,
            ],
            out_specs=[moved] * pieces,
            scratch_shapes=[pltpu.VMEM((rows, cols), jnp.float32)],
        ),
        compiler_params=pltpu.CompilerParams(vmem_limit_bytes=VMEM_LIMIT),
        cost_estimate=pl.CostEstimate(
            flops=flops, bytes_accessed=flops // 128, transcendentals=0
        ),
        name="expand_pieces",
    )(place, expand, got, vector, partner)


def split_halves(holding, which_dim, my_bit):
    first_half = lax.index_in_dim(holding, 0, which_dim, keepdims=False)
    second_half = lax.index_in_dim(holding, 1, which_dim, keepdims=False)
    kept_half = jnp.where(my_bit == 0, first_half, second_half)
    given_half = jnp.where(my_bit == 0, second_half, first_half)
    return (kept_half, given_half)


def reduce_bands(expansion, vector, low_bits, deg_index):
    slots, rows = expansion.shape[:2]
    holding = jnp.einsum("mrk,mkc->mrc", expansion, vector, preferred_element_type=jnp.float32)
    holding = holding.reshape((slots,) + (2,) * low_bits + (rows >> low_bits, vector.shape[2]))
    for bit in range(low_bits - 1, -1, -1):
        kept_half, given_half = split_halves(holding, 1, deg_index >> bit & 1)
        holding = kept_half + from_partner(given_half, "deg", 1 << bit)
    return holding.astype(jnp.bfloat16)


def body(spectral, wavenumbers, compress, section_own, section_peer, expand, block_ranks):
    deg_count = lax.axis_size("deg")
    zones = lax.axis_size("zonal")
    deg_index = lax.axis_index("deg")
    zone = lax.axis_index("zonal")
    levels_total = deg_count.bit_length() - 1
    low_bits = levels_total - SECTIONS
    slots = spectral.shape[0]
    cols = spectral.shape[2]
    rows = expand.shape[2]
    band = rows >> low_bits
    piece = band // zones
    pairwise = low_bits == 1 and zones <= 4 and piece % 16 == 0

    chunks = []
    first = 0
    for count in CHUNKS:
        chunks.append((first, count))
        first += count
    assert first == slots

    if pairwise:
        place = (deg_index & 1).astype(jnp.int32)[None]
        given = lax.dynamic_slice_in_dim(expand[:, 0], (1 - place[0]) * band, band, axis=1)
        got = from_partner(given, "deg", 1)
        out = jnp.zeros((zones * slots, piece, cols), jnp.bfloat16)
    else:
        out = []

    for first, count in chunks:
        vector = compress_slots(first, count, wavenumbers, block_ranks, spectral, compress)
        for section in range(1, SECTIONS + 1):
            partner = from_partner(vector, "deg", deg_count >> section)
            vector = section_slots(
                section, first, block_ranks, section_own, section_peer, vector, partner
            )
        if pairwise:
            partner = from_partner(vector, "deg", 1)
            parts = expand_pieces(first, place, expand, got, vector, partner, zones)
            for offset, part in enumerate(parts):
                if offset:
                    part = from_partner(part, "zonal", offset)
                out = lax.dynamic_update_slice(
                    out, part, ((zone ^ offset) * slots + first, 0, 0)
                )
        else:
            part = reduce_bands(expand[first : first + count, 0], vector, low_bits, deg_index)
            part = lax.all_to_all(part, "zonal", split_axis=1, concat_axis=0, tiled=True)
            out.append(part.reshape(zones, count, piece, cols))
    if not pairwise:
        out = jnp.concatenate(out, axis=1)
    return out.reshape(zones * slots, 1, 1, piece, cols)


def solution(mesh):
    in_specs = (
        P("zonal", "deg", None),
        P("zonal"),
        P("zonal", "deg", None),
        P(None, "zonal", "deg", None, None),
        P(None, "zonal", "deg", None, None),
        P("zonal", "deg", None, None),
        P(),
    )
    out_specs = P(None, "deg", "zonal", None, None)
    return jax.shard_map(body, mesh=mesh, in_specs=in_specs, out_specs=out_specs, check_vma=False)
```

```python
import functools
import math

import jax
import jax.numpy as jnp
from jax import lax
from jax.experimental import pallas as pl
from jax.experimental.pallas import tpu as pltpu
from jax.sharding import PartitionSpec as P

SECTIONS = 2
CHUNKS = (8, 8, 8, 8)
ORDER = (
    "C0",
    "C123",
    "G0",
    "10",
    "11",
    "20",
    "E0",
    "12",
    "21",
    "E1",
    "13",
    "22",
    "E2<P4_0",
    "23",
    "E3<P4_1",
)
COSTS = {}
VMEM_LIMIT = 52 * 2**20
EXPAND_LIMIT = 52 * 2**20
SECTION_LIMIT = 52 * 2**20
HBM = pl.BlockSpec(memory_space=pltpu.HBM)
ANY = pl.BlockSpec(memory_space=pl.ANY)


def from_partner(array, axis, offset, scope):
    pairs = [(i, i ^ offset) for i in range(lax.axis_size(axis))]
    with jax.named_scope(scope):
        return lax.ppermute(array, axis, pairs)


def dot(a, b, contract_a=1):
    return lax.dot_general(
        a, b, (((contract_a,), (0,)), ((), ())), preferred_element_type=jnp.float32
    )


def dot_pair(a, b, v, u):
    return dot(jnp.concatenate([a, b], axis=1), jnp.concatenate([v, u], axis=0))


def ordered(kernel, used, late):
    def run(*refs):
        kernel(*refs[:used], *refs[used + late :])

    return run


def call(kernel, name, scalars, operands, in_specs, out_specs, out_shape, steps, flops, late, scratch=(), limit=VMEM_LIMIT):
    return pl.pallas_call(
        ordered(kernel, len(scalars) + len(operands), len(late)),
        out_shape=out_shape,
        grid_spec=pltpu.PrefetchScalarGridSpec(
            num_scalar_prefetch=len(scalars),
            grid=(steps,),
            in_specs=[*in_specs] + [ANY] * len(late),
            out_specs=out_specs,
            scratch_shapes=scratch,
        ),
        compiler_params=pltpu.CompilerParams(vmem_limit_bytes=limit),
        cost_estimate=pl.CostEstimate(flops=flops, bytes_accessed=0, transcendentals=0),
        name=name,
    )(*scalars, *operands, *late)


def group(count, most=4):
    return max(b for b in range(1, most + 1) if count % b == 0)


def compress_kernel(first, b, waves, ranks, x_hbm, a_hbm, *refs):
    outs, (x_ref, a_ref, sems) = refs[:-3], refs[-3:]
    block = lax.axis_index("deg")
    nb, cols = x_ref.shape[1:]
    width = a_ref.shape[2]

    def copies(g):
        here, there = pl.ds(g * b, b), pl.ds(first + g * b, b)
        return (
            pltpu.make_async_copy(x_hbm.at[there], x_ref.at[here], sems.at[0, g]),
            pltpu.make_async_copy(a_hbm.at[there], a_ref.at[here], sems.at[1, g]),
        )

    for g in range(x_ref.shape[0] // b):
        for copy in copies(g):
            copy.start()
    degree = lax.broadcasted_iota(jnp.int32, (nb, cols), 0) + block * nb
    keep = lax.broadcasted_iota(jnp.int32, (width, cols), 0) < ranks[0, block]
    start = 0
    for out in outs:

        def some(g, carry, out=out, start=start):
            for copy in copies(start // b + g):
                copy.wait()
            for j in range(b):
                slot = g * b + j
                wave = waves[first + start + slot]
                live = jnp.where(degree >= wave, x_ref[start + slot], 0).astype(x_ref.dtype)
                total = dot(a_ref[start + slot], live, 0)
                out[slot] = jnp.where(keep, total, 0.0).astype(out.dtype)
            return carry

        lax.fori_loop(0, out.shape[0] // b, some, 0)
        start += out.shape[0]


def compress_slots(first, counts, waves, ranks, spectral, compress, late):
    b = min(group(count) for count in (first, *counts) if count)
    nb, cols = spectral.shape[1:]
    width = compress.shape[2]
    count = sum(counts)
    shapes = [(n, width, cols) for n in counts]
    return call(
        functools.partial(compress_kernel, first, b),
        "compress_slots",
        (waves, ranks),
        (spectral, compress),
        [HBM, HBM],
        [pl.BlockSpec(s, lambda i, *_: (0, 0, 0)) for s in shapes],
        [jax.ShapeDtypeStruct(s, jnp.bfloat16) for s in shapes],
        1,
        0 * count * nb * width * cols,
        late,
        [
            pltpu.VMEM((count, nb, cols), spectral.dtype),
            pltpu.VMEM((count, nb, width), compress.dtype),
            pltpu.SemaphoreType.DMA((2, count // b)),
        ],
    )


def section_kernel(section, b, ranks, own_ref, peer_ref, v_ref, u_ref, o_ref):
    block = lax.axis_index("deg")
    width, cols = v_ref.shape[1:]
    keep = lax.broadcasted_iota(jnp.int32, (width, cols), 0) < ranks[section, block]
    for j in range(b):
        total = dot_pair(own_ref[j], peer_ref[j], v_ref[j], u_ref[j])
        o_ref[j] = jnp.where(keep, total, 0.0).astype(o_ref.dtype)


def section_slots(section, first, ranks, own, peer, vector, partner, late, cost=0):
    count, width, cols = vector.shape
    b = group(math.gcd(first, count), 10)
    start = first // b
    weight = pl.BlockSpec(
        (None, b, None, width, width), lambda i, *_: (section - 1, start + i, 0, 0, 0)
    )
    part = pl.BlockSpec((b, width, cols), lambda i, *_: (i, 0, 0))
    return call(
        functools.partial(section_kernel, section, b),
        f"section_{section}_slots",
        (ranks,),
        (own, peer, vector, partner),
        [weight, weight, part, part],
        part,
        jax.ShapeDtypeStruct(vector.shape, jnp.bfloat16),
        count // b,
        cost or 4 * count * width * width * cols,
        late,
        (),
        SECTION_LIMIT,
    )


def expand_kernel(b, place, kept_ref, got_ref, both_ref, *refs):
    outs, rows_ref = refs[:-1], refs[-1]
    piece = outs[0].shape[1]
    zone = lax.axis_index("zonal")
    mine = place[0]
    for j in range(b):
        rows_ref[...] = dot_pair(kept_ref[j], got_ref[j], both_ref[mine, j], both_ref[1 - mine, j])
        for offset, out in enumerate(outs):
            at = pl.multiple_of((zone ^ offset) * piece, piece)
            out[j] = rows_ref[pl.ds(at, piece), :].astype(out.dtype)


def expand_pieces(first, place, expand, got, both, pieces, late):
    count, width, cols = both.shape[1:]
    rows = expand.shape[2] // 2
    piece = rows // pieces
    b = group(math.gcd(first, count), 4)
    start = first // b
    weight = pl.BlockSpec((b, None, rows, width), lambda i, p: (start + i, 0, p[0], 0))
    return call(
        functools.partial(expand_kernel, b),
        "expand_pieces",
        (place,),
        (expand, got, both),
        [weight, weight, pl.BlockSpec((2, b, width, cols), lambda i, *_: (0, i, 0, 0))],
        [pl.BlockSpec((b, piece, cols), lambda i, *_: (i, 0, 0))] * pieces,
        [jax.ShapeDtypeStruct((count, piece, cols), jnp.bfloat16)] * pieces,
        count // b,
        4 * count * rows * width * cols,
        late,
        [pltpu.VMEM((rows, cols), jnp.float32)],
        EXPAND_LIMIT,
    )


def split_halves(holding, which_dim, my_bit):
    first_half = lax.index_in_dim(holding, 0, which_dim, keepdims=False)
    second_half = lax.index_in_dim(holding, 1, which_dim, keepdims=False)
    kept_half = jnp.where(my_bit == 0, first_half, second_half)
    given_half = jnp.where(my_bit == 0, second_half, first_half)
    return (kept_half, given_half)


def reduce_bands(expansion, vector, low_bits, deg_index):
    slots, rows = expansion.shape[:2]
    holding = jnp.einsum("mrk,mkc->mrc", expansion, vector, preferred_element_type=jnp.float32)
    holding = holding.reshape((slots,) + (2,) * low_bits + (rows >> low_bits, vector.shape[2]))
    for bit in range(low_bits - 1, -1, -1):
        kept_half, given_half = split_halves(holding, 1, deg_index >> bit & 1)
        holding = kept_half + from_partner(given_half, "deg", 1 << bit, "band_halves")
    return holding.astype(jnp.bfloat16)


def body(spectral, wavenumbers, compress, section_own, section_peer, expand, block_ranks):
    deg_count = lax.axis_size("deg")
    zones = lax.axis_size("zonal")
    deg_index = lax.axis_index("deg")
    zone = lax.axis_index("zonal")
    levels_total = deg_count.bit_length() - 1
    low_bits = levels_total - SECTIONS
    slots = spectral.shape[0]
    cols = spectral.shape[2]
    rows = expand.shape[2]
    band = rows >> low_bits
    piece = band // zones
    pairwise = low_bits == 1 and zones == 4 and piece % 16 == 0

    firsts = [sum(CHUNKS[:k]) for k in range(len(CHUNKS))]
    assert sum(CHUNKS) == slots
    late, sent, state = [], {}, {}

    def gate(waits):
        return late[-1:] + [array for w in waits for array in sent[w]]

    def send(name, array, axis, offset):
        sent[name] = [from_partner(array, axis, offset, name)]
        return sent[name][0]

    def run(step, ks, waits):
        k = ks[0]
        first, count = firsts[k], CHUNKS[k]
        if step == "C":
            counts = [CHUNKS[k] for k in ks]
            outs = compress_slots(
                first, counts, wavenumbers, block_ranks, spectral, compress, gate(waits)
            )
            late.append(outs[-1])
            for k, out in zip(ks, outs):
                state[k] = out
                send(f"P1_{k}", out, "deg", deg_count >> 1)
        elif step in "12":
            section = int(step)
            out = section_slots(
                section, first, block_ranks, section_own, section_peer,
                state[k], sent[f"P{step}_{k}"][0], gate(waits), COSTS.get(f"{step}{k}", 0),
            )
            late.append(out)
            state[k] = out
            if section < SECTIONS:
                send(f"P{section + 1}_{k}", out, "deg", deg_count >> section + 1)
            elif pairwise:
                groups = [[i, i + 1] for i in range(0, deg_count, 2)]
                state[k] = lax.all_gather(out, "deg", axis_index_groups=groups)
        elif step == "G" and pairwise:
            send("PG_0", expand, "deg", 1)
        elif step == "E" and pairwise:
            parts = expand_pieces(
                first, place, expand, sent["PG_0"][0], state[k], zones, gate(waits)
            )
            late.append(parts[0])
            state[k] = parts
            sent[f"P4_{k}"] = [
                send(f"P4{offset}_{k}", part, "zonal", offset)
                for offset, part in enumerate(parts) if offset
            ]
        elif step == "E":
            part = reduce_bands(expand[first : first + count, 0], state[k], low_bits, deg_index)
            part = lax.all_to_all(part, "zonal", split_axis=1, concat_axis=0, tiled=True)
            state[k] = part.reshape(zones, count, piece, cols)

    if pairwise:
        place = (deg_index & 1).astype(jnp.int32)[None]
    for item in ORDER:
        step, _, waits = item.partition("<")
        with jax.named_scope("K" + step):
            run(step[0], [int(k) for k in step[1:]], waits.split(",") if waits and pairwise else [])

    if not pairwise:
        out = jnp.concatenate([state[k] for k in range(len(CHUNKS))], axis=1)
        return out.reshape(zones * slots, 1, 1, piece, cols)
    out = jnp.zeros((zones * slots, piece, cols), jnp.bfloat16)
    last = len(CHUNKS) - 1
    for k in [last, *range(last)]:
        at = zone * slots + firsts[k]
        out = lax.dynamic_update_slice(out, state[k][0], (at, 0, 0))
    for k in range(last + 1):
        for offset, part in enumerate(sent[f"P4_{k}"], 1):
            at = (zone ^ offset) * slots + firsts[k]
            out = lax.dynamic_update_slice(out, part, (at, 0, 0))
    return out.reshape(zones * slots, 1, 1, piece, cols)


def solution(mesh):
    in_specs = (
        P("zonal", "deg", None),
        P("zonal"),
        P("zonal", "deg", None),
        P(None, "zonal", "deg", None, None),
        P(None, "zonal", "deg", None, None),
        P("zonal", "deg", None, None),
        P(),
    )
    out_specs = P(None, "deg", "zonal", None, None)
    return jax.shard_map(body, mesh=mesh, in_specs=in_specs, out_specs=out_specs, check_vma=False)
```

```python
import functools
import math

import jax
import jax.numpy as jnp
from jax import lax
from jax.experimental import pallas as pl
from jax.experimental.pallas import tpu as pltpu
from jax.sharding import PartitionSpec as P

SECTIONS = 2
CHUNKS = (8, 8, 8, 8)
ORDER = (
    "C0",
    "C2",
    "G0",
    "C3<PG_0",
    "C1",
    "10",
    "11",
    "20",
    "E0+12",
    "21",
    "E1+13",
    "22",
    "E2+23<P4_0",
    "E3<P4_1",
)
COSTS = {}
VMEM_LIMIT = 832 * 2**16
HBM = pl.BlockSpec(memory_space=pltpu.HBM)
SMEM = pl.BlockSpec(memory_space=pltpu.SMEM)
ANY = pl.BlockSpec(memory_space=pl.ANY)


def from_partner(array, axis, offset, scope):
    pairs = [(i, i ^ offset) for i in range(lax.axis_size(axis))]
    with jax.named_scope(scope):
        return lax.ppermute(array, axis, pairs)


def dot(a, b, contract_a=1):
    return lax.dot_general(
        a, b, (((contract_a,), (0,)), ((), ())), preferred_element_type=jnp.float32
    )


def dot_pair(a, b, v, u):
    return dot(jnp.concatenate([a, b], axis=1), jnp.concatenate([v, u], axis=0))


def ordered(kernel, used, late):
    def run(*refs):
        kernel(*refs[:used], *refs[used + late :])

    return run


def group(count, most=4):
    return max(b for b in range(1, most + 1) if count % b == 0)


def compress_kernel(first, b, waves, ranks, x_hbm, a_hbm, *refs):
    outs, (x_ref, a_ref, sems) = refs[:-3], refs[-3:]
    block = lax.axis_index("deg")
    nb, cols = x_ref.shape[1:]
    width = a_ref.shape[2]

    def copies(g):
        here, there = pl.ds(g * b, b), pl.ds(first + g * b, b)
        return (
            pltpu.make_async_copy(x_hbm.at[there], x_ref.at[here], sems.at[0, g]),
            pltpu.make_async_copy(a_hbm.at[there], a_ref.at[here], sems.at[1, g]),
        )

    for g in range(x_ref.shape[0] // b):
        for copy in copies(g):
            copy.start()
    degree = lax.broadcasted_iota(jnp.int32, (nb, cols), 0) + block * nb
    keep = lax.broadcasted_iota(jnp.int32, (width, cols), 0) < ranks[0, block]
    start = 0
    for out in outs:

        def some(g, carry, out=out, start=start):
            for copy in copies(start // b + g):
                copy.wait()
            for j in range(b):
                slot = g * b + j
                wave = waves[first + start + slot]
                live = jnp.where(degree >= wave, x_ref[start + slot], 0).astype(x_ref.dtype)
                total = dot(a_ref[start + slot], live, 0)
                out[slot] = jnp.where(keep, total, 0.0).astype(out.dtype)
            return carry

        lax.fori_loop(0, out.shape[0] // b, some, 0)
        start += out.shape[0]


def compress_slots(first, counts, waves, ranks, spectral, compress, late):
    b = min(group(count) for count in (first, *counts) if count)
    nb, cols = spectral.shape[1:]
    width = compress.shape[2]
    count = sum(counts)
    shapes = [(n, width, cols) for n in counts]
    return pl.pallas_call(
        ordered(functools.partial(compress_kernel, first, b), 4, len(late)),
        out_shape=[jax.ShapeDtypeStruct(s, jnp.bfloat16) for s in shapes],
        grid=(1,),
        in_specs=[SMEM, SMEM, HBM, HBM] + [ANY] * len(late),
        out_specs=[pl.BlockSpec(s, lambda i: (0, 0, 0)) for s in shapes],
        scratch_shapes=[
            pltpu.VMEM((count, nb, cols), spectral.dtype),
            pltpu.VMEM((count, nb, width), compress.dtype),
            pltpu.SemaphoreType.DMA((2, count // b)),
        ],
        compiler_params=pltpu.CompilerParams(vmem_limit_bytes=VMEM_LIMIT),
        cost_estimate=pl.CostEstimate(flops=0, bytes_accessed=0, transcendentals=0),
        name="compress_slots",
    )(waves, ranks, spectral, compress, *late)


def section_task(section, first, ranks, own, peer, vector, partner):
    count, width, cols = vector.shape
    b = math.gcd(first, count)
    weight = (None, b, None, width, width)
    part = (b, width, cols)

    def kernel(i, ranks, own_ref, peer_ref, v_ref, u_ref, *outs):
        block = lax.axis_index("deg")
        keep = lax.broadcasted_iota(jnp.int32, (width, cols), 0) < ranks[section, block]
        for j in range(b):
            total = dot_pair(own_ref[j], peer_ref[j], v_ref[j], u_ref[j])
            total = jnp.where(keep, total, 0.0).astype(vector.dtype)
            outs[0][j] = total

    def weights(i):
        return (section - 1, first // b + i, 0, 0, 0)

    def parts(i):
        return (i, 0, 0)

    outs = [(jax.ShapeDtypeStruct(vector.shape, vector.dtype), part, parts)]
    ins = [(own, weight, weights), (peer, weight, weights)]
    ins += [(vector, part, parts), (partner, part, parts)]
    return kernel, ins, outs, count // b


def expand_task(first, expand, got, both, pieces):
    _, count, width, cols = both.shape
    b = group(math.gcd(first, count), 4)
    rows = expand.shape[2] // 2
    piece = rows // pieces
    block = (b, None, rows, width)

    def kernel(i, ranks, kept_ref, got_ref, both_ref, *outs):
        zone = lax.axis_index("zonal")
        mine = lax.axis_index("deg") % 2
        rows_ref = outs[-1]
        for j in range(b):
            rows_ref[...] = dot_pair(
                kept_ref[j], got_ref[j], both_ref[mine, j], both_ref[1 - mine, j]
            )
            for offset, out in enumerate(outs[:-1]):
                at = pl.multiple_of((zone ^ offset) * piece, piece)
                out[j] = rows_ref[pl.ds(at, piece), :].astype(out.dtype)

    def weights(i):
        return (first // b + i, 0, lax.axis_index("deg") % 2, 0)

    def parts(i):
        return (i, 0, 0)

    def pairs(i):
        return (0, i, 0, 0)

    shape = jax.ShapeDtypeStruct((count, piece, cols), jnp.bfloat16)
    outs = [(shape, (b, piece, cols), parts)] * pieces
    ins = [(expand, block, weights), (got, block, weights), (both, (2, b, width, cols), pairs)]
    return kernel, ins, outs, count // b


def fused(tasks, ranks, rows, cols, late, flops, held=()):
    starts = [sum(t[3] for t in tasks[:n]) for n in range(len(tasks))]
    ins, in_specs, outs, out_specs = [], [], [], []

    def spec(block, place_of, start, steps):
        def index(i):
            return place_of(jnp.clip(i - start, 0, steps - 1))

        return pl.BlockSpec(block, index)

    for (_, task_ins, task_outs, steps), start in zip(tasks, starts):
        for array, block, place_of in task_ins:
            ins.append(array)
            in_specs.append(spec(block, place_of, start, steps))
        for shape, block, place_of in task_outs:
            outs.append(shape)
            out_specs.append(spec(block, place_of, start, steps))

    def kernel(ranks, *refs):
        i = pl.program_id(0)
        sources = refs[: len(ins)]
        targets = refs[len(ins) + len(late) + len(held) : -1 - len(held)]
        for (run, task_ins, task_outs, steps), start in zip(tasks, starts):
            here, sources = sources[: len(task_ins)], sources[len(task_ins) :]
            there, targets = targets[: len(task_outs)], targets[len(task_outs) :]
            if len(task_outs) == 4:
                there = (*there, refs[-1])
            if len(tasks) == 1:
                run(i, ranks, *here, *there)
            else:

                @pl.when((i >= start) & (i < start + steps))
                def _():
                    run(i - start, ranks, *here, *there)

    return pl.pallas_call(
        kernel,
        out_shape=outs + [jax.ShapeDtypeStruct(h.shape, h.dtype) for h in held],
        grid=(sum(t[3] for t in tasks),),
        in_specs=[SMEM] + in_specs + [ANY] * (len(late) + len(held)),
        out_specs=out_specs + [ANY] * len(held),
        input_output_aliases={
            1 + len(ins) + len(late) + n: len(outs) + n for n in range(len(held))
        },
        scratch_shapes=[pltpu.VMEM((rows, cols), jnp.float32)],
        compiler_params=pltpu.CompilerParams(vmem_limit_bytes=VMEM_LIMIT),
        cost_estimate=pl.CostEstimate(flops=flops, bytes_accessed=0, transcendentals=0),
        name="butterfly_step",
    )(ranks, *ins, *late, *held)


def split_halves(holding, which_dim, my_bit):
    first_half = lax.index_in_dim(holding, 0, which_dim, keepdims=False)
    second_half = lax.index_in_dim(holding, 1, which_dim, keepdims=False)
    kept_half = jnp.where(my_bit == 0, first_half, second_half)
    given_half = jnp.where(my_bit == 0, second_half, first_half)
    return (kept_half, given_half)


def reduce_bands(expansion, vector, low_bits, deg_index):
    slots, rows = expansion.shape[:2]
    holding = jnp.einsum("mrk,mkc->mrc", expansion, vector, preferred_element_type=jnp.float32)
    holding = holding.reshape((slots,) + (2,) * low_bits + (rows >> low_bits, vector.shape[2]))
    for bit in range(low_bits - 1, -1, -1):
        kept_half, given_half = split_halves(holding, 1, deg_index >> bit & 1)
        holding = kept_half + from_partner(given_half, "deg", 1 << bit, "band_halves")
    return holding.astype(jnp.bfloat16)


def body(spectral, wavenumbers, compress, section_own, section_peer, expand, block_ranks):
    deg_count = lax.axis_size("deg")
    zones = lax.axis_size("zonal")
    deg_index = lax.axis_index("deg")
    zone = lax.axis_index("zonal")
    levels_total = deg_count.bit_length() - 1
    low_bits = levels_total - SECTIONS
    slots = spectral.shape[0]
    cols = spectral.shape[2]
    rows = expand.shape[2]
    band = rows >> low_bits
    piece = band // zones
    pairwise = low_bits == 1 and zones == 4 and piece % 16 == 0

    firsts = [sum(CHUNKS[:k]) for k in range(len(CHUNKS))]
    assert sum(CHUNKS) == slots
    late, sent, state = [], {}, {}

    def gate(waits):
        return late[-1:] + [array for w in waits for array in sent[w]]

    def send(name, array, axis, offset):
        sent[name] = [from_partner(array, axis, offset, name)]
        return sent[name][0]

    def gathered(k):
        part = reduce_bands(
            expand[firsts[k] : firsts[k] + CHUNKS[k], 0], state[k], low_bits, deg_index
        )
        part = lax.all_to_all(part, "zonal", split_axis=1, concat_axis=0, tiled=True)
        return part.reshape(zones, CHUNKS[k], piece, cols)

    def stepped(names, waits, hold):
        tasks = []
        for kind, k in names:
            if kind == "E":
                tasks.append(
                    expand_task(firsts[k], expand, sent["PG_0"][0], state[k], zones)
                )
            else:
                tasks.append(
                    section_task(
                        int(kind), firsts[k], block_ranks, section_own, section_peer,
                        state[k], sent[f"P{kind}_{k}"][0],
                    )
                )
        name = "+".join(kind + str(k) for kind, k in names)
        outs = [*fused(
            tasks, block_ranks, band, cols, gate(waits), COSTS.get(name, 0),
            [state[k] for k in hold],
        )]
        for k in hold[::-1]:
            state[k] = outs.pop()
        late.append(outs[0])
        for (kind, k), task in zip(names, tasks):
            made, outs = outs[: len(task[2])], outs[len(task[2]) :]
            if kind == "E":
                state[k] = made
                sent[f"P4_{k}"] = [
                    send(f"P4{offset}_{k}", part, "zonal", offset)
                    for offset, part in enumerate(made) if offset
                ]
            elif kind == "1":
                state[k] = made[0]
                send(f"P2_{k}", made[0], "deg", deg_count >> 2)
            elif pairwise:
                groups = [[i, i + 1] for i in range(0, deg_count, 2)]
                state[k] = lax.all_gather(made[0], "deg", axis_index_groups=groups)
            else:
                state[k] = made[0]

    for item in ORDER:
        names, _, waits = item.partition("<")
        names, _, hold = names.partition("^")
        hold = [int(k) for k in hold]
        waits = waits.split(",") if waits and pairwise else []
        with jax.named_scope("K" + names.replace("+", "_")):
            if names[0] == "C":
                ks = [int(k) for k in names[1:]]
                outs = compress_slots(
                    firsts[ks[0]], [CHUNKS[k] for k in ks], wavenumbers, block_ranks,
                    spectral, compress, gate(waits),
                )
                late.append(outs[-1])
                for k, out in zip(ks, outs):
                    state[k] = out
                    if not any(f"^{k}" in item for item in ORDER):
                        send(f"P1_{k}", out, "deg", deg_count >> 1)
            elif names[0] == "G":
                if pairwise:
                    send("PG_0", expand, "deg", 1)
            else:
                names = [(n[0], int(n[1])) for n in names.split("+")]
                for kind, k in names:
                    if kind == "E" and not pairwise:
                        state[k] = gathered(k)
                names = [n for n in names if pairwise or n[0] != "E"]
                if names:
                    stepped(names, waits, hold)
                    for k in hold:
                        send(f"P1_{k}", state[k], "deg", deg_count >> 1)

    if not pairwise:
        out = jnp.concatenate([state[k] for k in range(len(CHUNKS))], axis=1)
        return out.reshape(zones * slots, 1, 1, piece, cols)
    out = jnp.zeros((zones * slots, piece, cols), jnp.bfloat16)
    last = len(CHUNKS) - 1
    for k in [last, *range(last)]:
        at = zone * slots + firsts[k]
        out = lax.dynamic_update_slice(out, state[k][0], (at, 0, 0))
    for k in range(last + 1):
        for offset, part in enumerate(sent[f"P4_{k}"], 1):
            at = (zone ^ offset) * slots + firsts[k]
            out = lax.dynamic_update_slice(out, part, (at, 0, 0))
    return out.reshape(zones * slots, 1, 1, piece, cols)


def solution(mesh):
    in_specs = (
        P("zonal", "deg", None),
        P("zonal"),
        P("zonal", "deg", None),
        P(None, "zonal", "deg", None, None),
        P(None, "zonal", "deg", None, None),
        P("zonal", "deg", None, None),
        P(),
    )
    out_specs = P(None, "deg", "zonal", None, None)
    return jax.shard_map(body, mesh=mesh, in_specs=in_specs, out_specs=out_specs, check_vma=False)
```

```python
import functools
import math

import jax
import jax.numpy as jnp
from jax import lax
from jax.experimental import pallas as pl
from jax.experimental.pallas import tpu as pltpu
from jax.sharding import PartitionSpec as P

SECTIONS = 2
CHUNKS = (8, 8, 8, 8)
ORDER = (
    "C0",
    "C2",
    "G0",
    "C3<PG_0",
    "C1",
    "10",
    "11",
    "20",
    "E0",
    "12",
    "21",
    "E1+13",
    "22",
    "E2+23<P4_0",
    "E3<P4_1",
)
COSTS = {}
VMEM_LIMIT = 832 * 2**16
HBM = pl.BlockSpec(memory_space=pltpu.HBM)
SMEM = pl.BlockSpec(memory_space=pltpu.SMEM)
ANY = pl.BlockSpec(memory_space=pl.ANY)


def from_partner(array, axis, offset, scope):
    pairs = [(i, i ^ offset) for i in range(lax.axis_size(axis))]
    with jax.named_scope(scope):
        return lax.ppermute(array, axis, pairs)


def dot(a, b, contract_a=1):
    return lax.dot_general(
        a, b, (((contract_a,), (0,)), ((), ())), preferred_element_type=jnp.float32
    )


def dot_pair(a, b, v, u):
    return dot(jnp.concatenate([a, b], axis=1), jnp.concatenate([v, u], axis=0))


def ordered(kernel, used, late):
    def run(*refs):
        kernel(*refs[:used], *refs[used + late :])

    return run


def group(count, most=4):
    return max(b for b in range(1, most + 1) if count % b == 0)


def compress_kernel(first, b, waves_hbm, x_hbm, a_hbm, *refs):
    outs, (x_ref, a_ref, waves, sems, small) = refs[:-5], refs[-5:]
    block = lax.axis_index("deg")
    nb, cols = x_ref.shape[1:]

    def copies(g):
        here, there = pl.ds(g * b, b), pl.ds(first + g * b, b)
        return (
            pltpu.make_async_copy(x_hbm.at[there], x_ref.at[here], sems.at[0, g]),
            pltpu.make_async_copy(a_hbm.at[there], a_ref.at[here], sems.at[1, g]),
        )

    scalars = pltpu.make_async_copy(waves_hbm, waves, small.at[0])
    scalars.start()
    for g in range(x_ref.shape[0] // b):
        for copy in copies(g):
            copy.start()
    scalars.wait()
    degree = lax.broadcasted_iota(jnp.int32, (nb, cols), 0) + block * nb
    start = 0
    for out in outs:

        def some(g, carry, out=out, start=start):
            for copy in copies(start // b + g):
                copy.wait()
            for j in range(b):
                slot = g * b + j
                wave = waves[first + start + slot]
                live = jnp.where(degree >= wave, x_ref[start + slot], 0).astype(x_ref.dtype)
                total = dot(a_ref[start + slot], live, 0)
                out[slot] = total.astype(out.dtype)
            return carry

        lax.fori_loop(0, out.shape[0] // b, some, 0)
        start += out.shape[0]


def compress_slots(first, counts, waves, spectral, compress, late):
    b = min(group(count) for count in (first, *counts) if count)
    nb, cols = spectral.shape[1:]
    width = compress.shape[2]
    count = sum(counts)
    shapes = [(n, width, cols) for n in counts]
    return pl.pallas_call(
        ordered(functools.partial(compress_kernel, first, b), 3, len(late)),
        out_shape=[jax.ShapeDtypeStruct(s, jnp.bfloat16) for s in shapes],
        grid=(1,),
        in_specs=[HBM] * 3 + [ANY] * len(late),
        out_specs=[pl.BlockSpec(s, lambda i: (0, 0, 0)) for s in shapes],
        scratch_shapes=[
            pltpu.VMEM((count, nb, cols), spectral.dtype),
            pltpu.VMEM((count, nb, width), compress.dtype),
            pltpu.SMEM(waves.shape, waves.dtype),
            pltpu.SemaphoreType.DMA((2, count // b)),
            pltpu.SemaphoreType.DMA((1,)),
        ],
        compiler_params=pltpu.CompilerParams(vmem_limit_bytes=VMEM_LIMIT),
        cost_estimate=pl.CostEstimate(flops=0, bytes_accessed=0, transcendentals=0),
        name="compress_slots",
    )(waves, spectral, compress, *late)


def section_task(section, first, ranks, own, peer, vector, partner):
    count, width, cols = vector.shape
    b = math.gcd(first, count)
    weight = (None, b, None, width, width)
    part = (b, width, cols)

    def kernel(i, ranks, own_ref, peer_ref, v_ref, u_ref, *outs):
        block = lax.axis_index("deg")
        row = lax.broadcasted_iota(jnp.int32, (width, cols), 0)
        keep = row < ranks[section, block]
        if section == 1:
            partner_block = block ^ (lax.axis_size("deg") >> 1)
            keep_v, keep_u = row < ranks[0, block], row < ranks[0, partner_block]
        for j in range(b):
            v, u = v_ref[j], u_ref[j]
            if section == 1:
                v = jnp.where(keep_v, v, 0).astype(v.dtype)
                u = jnp.where(keep_u, u, 0).astype(u.dtype)
            total = dot_pair(own_ref[j], peer_ref[j], v, u)
            total = jnp.where(keep, total, 0.0).astype(vector.dtype)
            outs[0][j] = total

    def weights(i):
        return (section - 1, first // b + i, 0, 0, 0)

    def parts(i):
        return (i, 0, 0)

    outs = [(jax.ShapeDtypeStruct(vector.shape, vector.dtype), part, parts)]
    ins = [(own, weight, weights), (peer, weight, weights)]
    ins += [(vector, part, parts), (partner, part, parts)]
    return kernel, ins, outs, count // b


def expand_task(first, expand, got, both, pieces):
    _, count, width, cols = both.shape
    b = group(math.gcd(first, count), 4)
    rows = expand.shape[2] // 2
    piece = rows // pieces
    block = (b, None, rows, width)

    def kernel(i, ranks, kept_ref, got_ref, both_ref, *outs):
        zone = lax.axis_index("zonal")
        mine = lax.axis_index("deg") % 2
        rows_ref = outs[-1]
        for j in range(b):
            total = dot_pair(
                kept_ref[j], got_ref[j], both_ref[mine, j], both_ref[1 - mine, j]
            )
            rows_ref[...] = total.astype(rows_ref.dtype)
            for offset, out in enumerate(outs[:-1]):
                at = pl.multiple_of((zone ^ offset) * piece, piece)
                out[j] = rows_ref[pl.ds(at, piece), :]

    def weights(i):
        return (first // b + i, 0, lax.axis_index("deg") % 2, 0)

    def parts(i):
        return (i, 0, 0)

    def pairs(i):
        return (0, i, 0, 0)

    shape = jax.ShapeDtypeStruct((count, piece, cols), jnp.bfloat16)
    outs = [(shape, (b, piece, cols), parts)] * pieces
    ins = [(expand, block, weights), (got, block, weights), (both, (2, b, width, cols), pairs)]
    return kernel, ins, outs, count // b


def fused(tasks, ranks, rows, cols, late, flops, held=()):
    starts = [sum(t[3] for t in tasks[:n]) for n in range(len(tasks))]
    ins, in_specs, outs, out_specs = [], [], [], []

    def spec(block, place_of, start, steps):
        def index(i):
            return place_of(jnp.clip(i - start, 0, steps - 1))

        return pl.BlockSpec(block, index)

    for (_, task_ins, task_outs, steps), start in zip(tasks, starts):
        for array, block, place_of in task_ins:
            ins.append(array)
            in_specs.append(spec(block, place_of, start, steps))
        for shape, block, place_of in task_outs:
            outs.append(shape)
            out_specs.append(spec(block, place_of, start, steps))

    def kernel(ranks, *refs):
        i = pl.program_id(0)
        sources = refs[: len(ins)]
        targets = refs[len(ins) + len(late) + len(held) : -1 - len(held)]
        for (run, task_ins, task_outs, steps), start in zip(tasks, starts):
            here, sources = sources[: len(task_ins)], sources[len(task_ins) :]
            there, targets = targets[: len(task_outs)], targets[len(task_outs) :]
            if len(task_outs) == 4:
                there = (*there, refs[-1])
            if len(tasks) == 1:
                run(i, ranks, *here, *there)
            else:

                @pl.when((i >= start) & (i < start + steps))
                def _():
                    run(i - start, ranks, *here, *there)

    return pl.pallas_call(
        kernel,
        out_shape=outs + [jax.ShapeDtypeStruct(h.shape, h.dtype) for h in held],
        grid=(sum(t[3] for t in tasks),),
        in_specs=[SMEM] + in_specs + [ANY] * (len(late) + len(held)),
        out_specs=out_specs + [ANY] * len(held),
        input_output_aliases={
            1 + len(ins) + len(late) + n: len(outs) + n for n in range(len(held))
        },
        scratch_shapes=[pltpu.VMEM((rows, cols), jnp.bfloat16)],
        compiler_params=pltpu.CompilerParams(vmem_limit_bytes=VMEM_LIMIT),
        cost_estimate=pl.CostEstimate(flops=flops, bytes_accessed=0, transcendentals=0),
        name="butterfly_step",
    )(ranks, *ins, *late, *held)


def split_halves(holding, which_dim, my_bit):
    first_half = lax.index_in_dim(holding, 0, which_dim, keepdims=False)
    second_half = lax.index_in_dim(holding, 1, which_dim, keepdims=False)
    kept_half = jnp.where(my_bit == 0, first_half, second_half)
    given_half = jnp.where(my_bit == 0, second_half, first_half)
    return (kept_half, given_half)


def reduce_bands(expansion, vector, low_bits, deg_index):
    slots, rows = expansion.shape[:2]
    holding = jnp.einsum("mrk,mkc->mrc", expansion, vector, preferred_element_type=jnp.float32)
    holding = holding.reshape((slots,) + (2,) * low_bits + (rows >> low_bits, vector.shape[2]))
    for bit in range(low_bits - 1, -1, -1):
        kept_half, given_half = split_halves(holding, 1, deg_index >> bit & 1)
        holding = kept_half + from_partner(given_half, "deg", 1 << bit, "band_halves")
    return holding.astype(jnp.bfloat16)


def body(spectral, wavenumbers, compress, section_own, section_peer, expand, block_ranks):
    deg_count = lax.axis_size("deg")
    zones = lax.axis_size("zonal")
    deg_index = lax.axis_index("deg")
    zone = lax.axis_index("zonal")
    levels_total = deg_count.bit_length() - 1
    low_bits = levels_total - SECTIONS
    slots = spectral.shape[0]
    cols = spectral.shape[2]
    rows = expand.shape[2]
    band = rows >> low_bits
    piece = band // zones
    pairwise = low_bits == 1 and zones == 4 and piece % 16 == 0

    firsts = [sum(CHUNKS[:k]) for k in range(len(CHUNKS))]
    assert sum(CHUNKS) == slots
    late, sent, state = [], {}, {}

    def gate(waits):
        return late[-1:] + [array for w in waits for array in sent[w]]

    def send(name, array, axis, offset):
        sent[name] = [from_partner(array, axis, offset, name)]
        return sent[name][0]

    def gathered(k):
        part = reduce_bands(
            expand[firsts[k] : firsts[k] + CHUNKS[k], 0], state[k], low_bits, deg_index
        )
        part = lax.all_to_all(part, "zonal", split_axis=1, concat_axis=0, tiled=True)
        return part.reshape(zones, CHUNKS[k], piece, cols)

    def stepped(names, waits, hold):
        tasks = []
        for kind, k in names:
            if kind == "E":
                tasks.append(
                    expand_task(firsts[k], expand, sent["PG_0"][0], state[k], zones)
                )
            else:
                tasks.append(
                    section_task(
                        int(kind), firsts[k], block_ranks, section_own, section_peer,
                        state[k], sent[f"P{kind}_{k}"][0],
                    )
                )
        name = "+".join(kind + str(k) for kind, k in names)
        outs = [*fused(
            tasks, block_ranks, band, cols, gate(waits), COSTS.get(name, 0),
            [state[k] for k in hold],
        )]
        for k in hold[::-1]:
            state[k] = outs.pop()
        late.append(outs[0])
        for (kind, k), task in zip(names, tasks):
            made, outs = outs[: len(task[2])], outs[len(task[2]) :]
            if kind == "E":
                state[k] = made
                sent[f"P4_{k}"] = [
                    send(f"P4{offset}_{k}", part, "zonal", offset)
                    for offset, part in enumerate(made) if offset
                ]
            elif kind == "1":
                state[k] = made[0]
                send(f"P2_{k}", made[0], "deg", deg_count >> 2)
            elif pairwise:
                groups = [[i, i + 1] for i in range(0, deg_count, 2)]
                state[k] = lax.all_gather(made[0], "deg", axis_index_groups=groups)
            else:
                state[k] = made[0]

    for item in ORDER:
        names, _, waits = item.partition("<")
        names, _, hold = names.partition("^")
        hold = [int(k) for k in hold]
        waits = waits.split(",") if waits and pairwise else []
        with jax.named_scope("K" + names.replace("+", "_")):
            if names[0] == "C":
                ks = [int(k) for k in names[1:]]
                outs = compress_slots(
                    firsts[ks[0]], [CHUNKS[k] for k in ks], wavenumbers,
                    spectral, compress, gate(waits),
                )
                late.append(outs[-1])
                for k, out in zip(ks, outs):
                    state[k] = out
                    if not any(f"^{k}" in item for item in ORDER):
                        send(f"P1_{k}", out, "deg", deg_count >> 1)
            elif names[0] == "G":
                if pairwise:
                    send("PG_0", expand, "deg", 1)
            else:
                names = [(n[0], int(n[1])) for n in names.split("+")]
                for kind, k in names:
                    if kind == "E" and not pairwise:
                        state[k] = gathered(k)
                names = [n for n in names if pairwise or n[0] != "E"]
                if names:
                    stepped(names, waits, hold)
                    for k in hold:
                        send(f"P1_{k}", state[k], "deg", deg_count >> 1)

    if not pairwise:
        out = jnp.concatenate([state[k] for k in range(len(CHUNKS))], axis=1)
        return out.reshape(zones * slots, 1, 1, piece, cols)
    out = jnp.zeros((zones * slots, piece, cols), jnp.bfloat16)
    last = len(CHUNKS) - 1
    for k in [last, *range(last)]:
        at = zone * slots + firsts[k]
        out = lax.dynamic_update_slice(out, state[k][0], (at, 0, 0))
    for k in range(last + 1):
        for offset, part in enumerate(sent[f"P4_{k}"], 1):
            at = (zone ^ offset) * slots + firsts[k]
            out = lax.dynamic_update_slice(out, part, (at, 0, 0))
    return out.reshape(zones * slots, 1, 1, piece, cols)


def solution(mesh):
    in_specs = (
        P("zonal", "deg", None),
        P("zonal"),
        P("zonal", "deg", None),
        P(None, "zonal", "deg", None, None),
        P(None, "zonal", "deg", None, None),
        P("zonal", "deg", None, None),
        P(),
    )
    out_specs = P(None, "deg", "zonal", None, None)
    return jax.shard_map(body, mesh=mesh, in_specs=in_specs, out_specs=out_specs, check_vma=False)
```

```python
import functools
import math

import jax
import jax.numpy as jnp
from jax import lax
from jax.experimental import pallas as pl
from jax.experimental.pallas import tpu as pltpu
from jax.sharding import PartitionSpec as P

SECTIONS = 2
CHUNKS = (8, 8, 8, 8)
ORDER = (
    "C0",
    "C2",
    "G0",
    "C3<PG_0",
    "C1",
    "10",
    "11",
    "20",
    "E0",
    "12",
    "21",
    "E1+13",
    "22<P4_0",
    "E2+23",
    "E3<P4_1",
)
COSTS = {}
VMEM_LIMIT = 832 * 2**16
HBM = pl.BlockSpec(memory_space=pltpu.HBM)
SMEM = pl.BlockSpec(memory_space=pltpu.SMEM)
ANY = pl.BlockSpec(memory_space=pl.ANY)


def from_partner(array, axis, offset, scope):
    pairs = [(i, i ^ offset) for i in range(lax.axis_size(axis))]
    with jax.named_scope(scope):
        return lax.ppermute(array, axis, pairs)


def dot(a, b, contract_a=1):
    return lax.dot_general(
        a, b, (((contract_a,), (0,)), ((), ())), preferred_element_type=jnp.float32
    )


def dot_pair(a, b, v, u):
    return dot(jnp.concatenate([a, b], axis=1), jnp.concatenate([v, u], axis=0))


def ordered(kernel, used, late):
    def run(*refs):
        kernel(*refs[:used], *refs[used + late :])

    return run


def group(count, most=4):
    return max(b for b in range(1, most + 1) if count % b == 0)


def compress_kernel(first, b, waves_hbm, x_hbm, a_hbm, *refs):
    outs, (x_ref, a_ref, waves, sems, small) = refs[:-5], refs[-5:]
    block = lax.axis_index("deg")
    nb, cols = x_ref.shape[1:]

    def copies(g):
        here, there = pl.ds(g * b, b), pl.ds(first + g * b, b)
        return (
            pltpu.make_async_copy(x_hbm.at[there], x_ref.at[here], sems.at[0, g]),
            pltpu.make_async_copy(a_hbm.at[there], a_ref.at[here], sems.at[1, g]),
        )

    scalars = pltpu.make_async_copy(waves_hbm, waves, small.at[0])
    scalars.start()
    for g in range(x_ref.shape[0] // b):
        for copy in copies(g):
            copy.start()
    scalars.wait()
    degree = lax.broadcasted_iota(jnp.int32, (nb, cols), 0) + block * nb
    start = 0
    for out in outs:

        def some(g, carry, out=out, start=start):
            for copy in copies(start // b + g):
                copy.wait()
            for j in range(b):
                slot = g * b + j
                wave = waves[first + start + slot]
                live = jnp.where(degree >= wave, x_ref[start + slot], 0).astype(x_ref.dtype)
                total = dot(a_ref[start + slot], live, 0)
                out[slot] = total.astype(out.dtype)
            return carry

        lax.fori_loop(0, out.shape[0] // b, some, 0)
        start += out.shape[0]


def compress_slots(first, counts, waves, spectral, compress, late):
    b = min(group(count) for count in (first, *counts) if count)
    nb, cols = spectral.shape[1:]
    width = compress.shape[2]
    count = sum(counts)
    shapes = [(n, width, cols) for n in counts]
    return pl.pallas_call(
        ordered(functools.partial(compress_kernel, first, b), 3, len(late)),
        out_shape=[jax.ShapeDtypeStruct(s, jnp.bfloat16) for s in shapes],
        grid=(1,),
        in_specs=[HBM] * 3 + [ANY] * len(late),
        out_specs=[pl.BlockSpec(s, lambda i: (0, 0, 0)) for s in shapes],
        scratch_shapes=[
            pltpu.VMEM((count, nb, cols), spectral.dtype),
            pltpu.VMEM((count, nb, width), compress.dtype),
            pltpu.SMEM(waves.shape, waves.dtype),
            pltpu.SemaphoreType.DMA((2, count // b)),
            pltpu.SemaphoreType.DMA((1,)),
        ],
        compiler_params=pltpu.CompilerParams(vmem_limit_bytes=VMEM_LIMIT),
        cost_estimate=pl.CostEstimate(flops=0, bytes_accessed=0, transcendentals=0),
        name="compress_slots",
    )(waves, spectral, compress, *late)


def section_task(section, first, ranks, own, peer, vector, partner):
    count, width, cols = vector.shape
    b = math.gcd(first, count)
    weight = (None, b, None, width, width)
    part = (b, width, cols)

    def kernel(i, ranks, own_ref, peer_ref, v_ref, u_ref, *outs):
        block = lax.axis_index("deg")
        row = lax.broadcasted_iota(jnp.int32, (width, cols), 0)
        keep = row < ranks[section, block]
        if section == 1:
            partner_block = block ^ (lax.axis_size("deg") >> 1)
            keep_v, keep_u = row < ranks[0, block], row < ranks[0, partner_block]
        for j in range(b):
            v, u = v_ref[j], u_ref[j]
            if section == 1:
                v = jnp.where(keep_v, v, 0).astype(v.dtype)
                u = jnp.where(keep_u, u, 0).astype(u.dtype)
            total = dot_pair(own_ref[j], peer_ref[j], v, u)
            total = jnp.where(keep, total, 0.0).astype(vector.dtype)
            outs[0][j] = total

    def weights(i):
        return (section - 1, first // b + i, 0, 0, 0)

    def parts(i):
        return (i, 0, 0)

    outs = [(jax.ShapeDtypeStruct(vector.shape, vector.dtype), part, parts)]
    ins = [(own, weight, weights), (peer, weight, weights)]
    ins += [(vector, part, parts), (partner, part, parts)]
    return kernel, ins, outs, count // b


def expand_task(first, expand, got, both, pieces):
    _, count, width, cols = both.shape
    b = group(math.gcd(first, count), 4)
    rows = expand.shape[2] // 2
    piece = rows // pieces
    block = (b, None, rows, width)

    def kernel(i, ranks, kept_ref, got_ref, both_ref, *outs):
        zone = lax.axis_index("zonal")
        mine = lax.axis_index("deg") % 2
        rows_ref = outs[-1]
        for j in range(b):
            total = dot_pair(
                kept_ref[j], got_ref[j], both_ref[mine, j], both_ref[1 - mine, j]
            )
            rows_ref[...] = total.astype(rows_ref.dtype)
            for offset, out in enumerate(outs[:-1]):
                at = pl.multiple_of((zone ^ offset) * piece, piece)
                out[j] = rows_ref[pl.ds(at, piece), :]

    def weights(i):
        return (first // b + i, 0, lax.axis_index("deg") % 2, 0)

    def parts(i):
        return (i, 0, 0)

    def pairs(i):
        return (0, i, 0, 0)

    shape = jax.ShapeDtypeStruct((count, piece, cols), jnp.bfloat16)
    outs = [(shape, (b, piece, cols), parts)] * pieces
    ins = [(expand, block, weights), (got, block, weights), (both, (2, b, width, cols), pairs)]
    return kernel, ins, outs, count // b


def fused(tasks, ranks, rows, cols, late, flops, held=()):
    starts = [sum(t[3] for t in tasks[:n]) for n in range(len(tasks))]
    ins, in_specs, outs, out_specs = [], [], [], []

    def spec(block, place_of, start, steps):
        def index(i):
            return place_of(jnp.clip(i - start, 0, steps - 1))

        return pl.BlockSpec(block, index)

    for (_, task_ins, task_outs, steps), start in zip(tasks, starts):
        for array, block, place_of in task_ins:
            ins.append(array)
            in_specs.append(spec(block, place_of, start, steps))
        for shape, block, place_of in task_outs:
            outs.append(shape)
            out_specs.append(spec(block, place_of, start, steps))

    def kernel(ranks, *refs):
        i = pl.program_id(0)
        sources = refs[: len(ins)]
        targets = refs[len(ins) + len(late) + len(held) : -1 - len(held)]
        for (run, task_ins, task_outs, steps), start in zip(tasks, starts):
            here, sources = sources[: len(task_ins)], sources[len(task_ins) :]
            there, targets = targets[: len(task_outs)], targets[len(task_outs) :]
            if len(task_outs) == 4:
                there = (*there, refs[-1])
            if len(tasks) == 1:
                run(i, ranks, *here, *there)
            else:

                @pl.when((i >= start) & (i < start + steps))
                def _():
                    run(i - start, ranks, *here, *there)

    return pl.pallas_call(
        kernel,
        out_shape=outs + [jax.ShapeDtypeStruct(h.shape, h.dtype) for h in held],
        grid=(sum(t[3] for t in tasks),),
        in_specs=[SMEM] + in_specs + [ANY] * (len(late) + len(held)),
        out_specs=out_specs + [ANY] * len(held),
        input_output_aliases={
            1 + len(ins) + len(late) + n: len(outs) + n for n in range(len(held))
        },
        scratch_shapes=[pltpu.VMEM((rows, cols), jnp.bfloat16)],
        compiler_params=pltpu.CompilerParams(vmem_limit_bytes=VMEM_LIMIT),
        cost_estimate=pl.CostEstimate(flops=flops, bytes_accessed=0, transcendentals=0),
        name="butterfly_step",
    )(ranks, *ins, *late, *held)


def split_halves(holding, which_dim, my_bit):
    first_half = lax.index_in_dim(holding, 0, which_dim, keepdims=False)
    second_half = lax.index_in_dim(holding, 1, which_dim, keepdims=False)
    kept_half = jnp.where(my_bit == 0, first_half, second_half)
    given_half = jnp.where(my_bit == 0, second_half, first_half)
    return (kept_half, given_half)


def reduce_bands(expansion, vector, low_bits, deg_index):
    slots, rows = expansion.shape[:2]
    holding = jnp.einsum("mrk,mkc->mrc", expansion, vector, preferred_element_type=jnp.float32)
    holding = holding.reshape((slots,) + (2,) * low_bits + (rows >> low_bits, vector.shape[2]))
    for bit in range(low_bits - 1, -1, -1):
        kept_half, given_half = split_halves(holding, 1, deg_index >> bit & 1)
        holding = kept_half + from_partner(given_half, "deg", 1 << bit, "band_halves")
    return holding.astype(jnp.bfloat16)


def body(spectral, wavenumbers, compress, section_own, section_peer, expand, block_ranks):
    deg_count = lax.axis_size("deg")
    zones = lax.axis_size("zonal")
    deg_index = lax.axis_index("deg")
    zone = lax.axis_index("zonal")
    levels_total = deg_count.bit_length() - 1
    low_bits = levels_total - SECTIONS
    slots = spectral.shape[0]
    cols = spectral.shape[2]
    rows = expand.shape[2]
    band = rows >> low_bits
    piece = band // zones
    pairwise = low_bits == 1 and zones == 4 and piece % 16 == 0

    firsts = [sum(CHUNKS[:k]) for k in range(len(CHUNKS))]
    assert sum(CHUNKS) == slots
    late, sent, state = [], {}, {}

    def gate(waits):
        return late[-1:] + [array for w in waits for array in sent[w]]

    def send(name, array, axis, offset):
        sent[name] = [from_partner(array, axis, offset, name)]
        return sent[name][0]

    def gathered(k):
        part = reduce_bands(
            expand[firsts[k] : firsts[k] + CHUNKS[k], 0], state[k], low_bits, deg_index
        )
        part = lax.all_to_all(part, "zonal", split_axis=1, concat_axis=0, tiled=True)
        return part.reshape(zones, CHUNKS[k], piece, cols)

    def stepped(names, waits, hold):
        tasks = []
        for kind, k in names:
            if kind == "E":
                tasks.append(
                    expand_task(firsts[k], expand, sent["PG_0"][0], state[k], zones)
                )
            else:
                tasks.append(
                    section_task(
                        int(kind), firsts[k], block_ranks, section_own, section_peer,
                        state[k], sent[f"P{kind}_{k}"][0],
                    )
                )
        name = "+".join(kind + str(k) for kind, k in names)
        outs = [*fused(
            tasks, block_ranks, band, cols, gate(waits), COSTS.get(name, 0),
            [state[k] for k in hold],
        )]
        for k in hold[::-1]:
            state[k] = outs.pop()
        late.append(outs[0])
        for (kind, k), task in zip(names, tasks):
            made, outs = outs[: len(task[2])], outs[len(task[2]) :]
            if kind == "E":
                state[k] = made
                sent[f"P4_{k}"] = [
                    send(f"P4{offset}_{k}", part, "zonal", offset)
                    for offset, part in enumerate(made) if offset
                ]
            elif kind == "1":
                state[k] = made[0]
                send(f"P2_{k}", made[0], "deg", deg_count >> 2)
            elif pairwise:
                groups = [[i, i + 1] for i in range(0, deg_count, 2)]
                state[k] = lax.all_gather(made[0], "deg", axis_index_groups=groups)
            else:
                state[k] = made[0]

    for item in ORDER:
        names, _, waits = item.partition("<")
        names, _, hold = names.partition("^")
        hold = [int(k) for k in hold]
        waits = waits.split(",") if waits and pairwise else []
        with jax.named_scope("K" + names.replace("+", "_")):
            if names[0] == "C":
                ks = [int(k) for k in names[1:]]
                outs = compress_slots(
                    firsts[ks[0]], [CHUNKS[k] for k in ks], wavenumbers,
                    spectral, compress, gate(waits),
                )
                late.append(outs[-1])
                for k, out in zip(ks, outs):
                    state[k] = out
                    if not any(f"^{k}" in item for item in ORDER):
                        send(f"P1_{k}", out, "deg", deg_count >> 1)
            elif names[0] == "G":
                if pairwise:
                    send("PG_0", expand, "deg", 1)
            else:
                names = [(n[0], int(n[1])) for n in names.split("+")]
                for kind, k in names:
                    if kind == "E" and not pairwise:
                        state[k] = gathered(k)
                names = [n for n in names if pairwise or n[0] != "E"]
                if names:
                    stepped(names, waits, hold)
                    for k in hold:
                        send(f"P1_{k}", state[k], "deg", deg_count >> 1)

    if not pairwise:
        out = jnp.concatenate([state[k] for k in range(len(CHUNKS))], axis=1)
        return out.reshape(zones * slots, 1, 1, piece, cols)
    out = jnp.zeros((zones * slots, piece, cols), jnp.bfloat16)
    last = len(CHUNKS) - 1
    for k in [last, *range(last)]:
        at = zone * slots + firsts[k]
        out = lax.dynamic_update_slice(out, state[k][0], (at, 0, 0))
    for k in range(last + 1):
        for offset, part in enumerate(sent[f"P4_{k}"], 1):
            at = (zone ^ offset) * slots + firsts[k]
            out = lax.dynamic_update_slice(out, part, (at, 0, 0))
    return out.reshape(zones * slots, 1, 1, piece, cols)


def solution(mesh):
    in_specs = (
        P("zonal", "deg", None),
        P("zonal"),
        P("zonal", "deg", None),
        P(None, "zonal", "deg", None, None),
        P(None, "zonal", "deg", None, None),
        P("zonal", "deg", None, None),
        P(),
    )
    out_specs = P(None, "deg", "zonal", None, None)
    return jax.shard_map(body, mesh=mesh, in_specs=in_specs, out_specs=out_specs, check_vma=False)
```
